32 devices in a mesh: shard: 4 (over y, x), context: 4 (over z), tensor: 2 (over core).
Axes of the slice: x: 2, y: 2, z: 4, core: 2. Of those that a mesh axis runs over, the one named last changes fastest.
Arguments:
- inputs: bfloat16 [64, 512, 1024], P('shard', 'context'), may hold values from -6 to 6
- lengths: int32 [64], P('shard'), may hold values from 1 to 512, as said below
- w_qkv: bfloat16 [3, 1024, 1024], P(None, ('shard', 'context'), 'tensor'), may hold values from -0.1875 to 0.1875
- b_qv: float32 [2, 1024], P(None, 'tensor'), may hold values from -1.5 to 1.5
- w_out: bfloat16 [1024, 1024], P('tensor', ('shard', 'context')), may hold values from -1 to 1
- b_out: float32 [1024], replicated, may hold values from -1.5 to 1.5
- w_up: bfloat16 [1024, 4096], P(('shard', 'context'), 'tensor'), may hold values from -0.1875 to 0.1875
- b_up: float32 [4096], P('tensor'), may hold values from -1.5 to 1.5
- w_down: bfloat16 [4096, 1024], P('tensor', ('shard', 'context')), may hold values from -0.09375 to 0.09375
- down_bias: float32 [1024], replicated, may hold values from -1.5 to 1.5
- gain_attn: float32 [1024], replicated, may hold values from 0.1 to 1.9
- shift_attn: float32 [1024], replicated, may hold values from -1.5 to 1.5
- gain_ffn: float32 [1024], replicated, may hold values from 0.1 to 1.9
- shift_ffn: float32 [1024], replicated, may hold values from -1.5 to 1.5
- grad_output: bfloat16 [64, 512, 1024], P('shard', 'context'), may hold values from -6 to 6
Outputs:
- outputs: bfloat16 [64, 512, 1024], P('shard', 'context')
- grad_inputs: bfloat16 [64, 512, 1024], P('shard', 'context')
- grad_w_qkv: float32 [3, 1024, 1024], P(None, ('shard', 'context'), 'tensor')
- grad_b_qv: float32 [2, 1024], P(None, 'tensor')
- grad_w_out: float32 [1024, 1024], P('tensor', ('shard', 'context'))
- grad_b_out: float32 [1024], replicated
- grad_w_up: float32 [1024, 4096], P(('shard', 'context'), 'tensor')
- up_bias_gradient: float32 [4096], P('tensor')
- grad_w_down: float32 [4096, 1024], P('tensor', ('shard', 'context'))
- grad_b_down: float32 [1024], replicated
- grad_gain_attn: float32 [1024], replicated
- grad_shift_attn: float32 [1024], replicated
- grad_gain_ffn: float32 [1024], replicated
- grad_shift_ffn: float32 [1024], replicated
The draws below stay inside these ranges and needn't reach their ends.
Inputs may be any that keep to these rules, and one draw needn't show every extreme that they name: In every group of 16 sequences along the shard axis, one has length 512; group lengths differ in their lower range.
All inputs are finite; a program needn't handle non-finite values.
Results may differ from the reference program's by a relative error of at most 0.02.
Values may be sent and summed in bfloat16 or wider, within the bound.
A program may use at most 192 MiB of HBM per device.

```python
import jax
import jax.numpy as jnp
from jax import lax

D = 1024
HEADS = 16
HEAD_DIM = 64
FF = 4096
LEN = 512
SEQ_G = 16
SEQS = 64


def draw_lengths(key, part):
    key = jax.random.fold_in(key, 7)
    key_low, key_len, key_selection = jax.random.split(key, 3)
    groups = SEQS // SEQ_G
    lower_end = jax.random.randint(key_low, (groups, 1), 1, LEN // 2 + 1)
    drawn = jax.random.randint(key_len, (groups, SEQ_G), lower_end, LEN + 1)
    picked = jax.random.randint(key_selection, (groups, 1), 0, SEQ_G)
    slots = jnp.arange(SEQ_G, dtype=jnp.int32)[None, :]
    drawn = jnp.where(slots == picked, LEN, drawn)
    return drawn.reshape(SEQS).astype(jnp.int32)


def levels(own_key, dims, shards, smallest, largest):
    factor_of = 1.0
    for position, blocks in shards:
        draws = jax.random.uniform(jax.random.fold_in(jax.random.fold_in(own_key, 6), position), (blocks,), jnp.float32, smallest / len(shards), largest / len(shards))
        factor_of = factor_of * jnp.repeat(jnp.exp(draws), dims[position] // blocks).reshape((-1,) + (1,) * (len(dims) - 1 - position))
    return factor_of


def noise(key, extent, scale, most, pieces=(), kind=jnp.bfloat16):
    array = scale * jax.random.normal(key, extent, jnp.float32)
    if pieces:
        array = array * levels(key, extent, pieces, -0.22, 0.18)
    return jnp.clip(array, -most, most).astype(kind)


def setup_inputs(seed: int = 0) -> dict:
    key_list = jax.random.split(jax.random.key(seed), 16)
    return {
        "inputs": noise(key_list[0], (SEQS, LEN, D), 1.0, 6.0, ((0, 4), (1, 4))),
        "lengths": draw_lengths(jax.random.fold_in(key_list[15], 71), 0),
        "w_qkv": noise(key_list[2], (3, D, D), D ** -0.5, 0.1875, ((1, 16), (2, 2))),
        "b_qv": noise(key_list[3], (2, D), 0.3, 1.5, ((1, 2),), jnp.float32),
        "w_out": noise(key_list[4], (D, D), (D // 32) ** -0.5, 1.0, ((0, 2), (1, 16))),
        "b_out": noise(key_list[5], (D,), 0.3, 1.5, (), jnp.float32),
        "w_up": noise(key_list[6], (D, FF), D ** -0.5, 0.1875, ((0, 16), (1, 2))),
        "b_up": noise(key_list[7], (FF,), 0.3, 1.5, ((0, 2),), jnp.float32),
        "w_down": noise(key_list[8], (FF, D), FF ** -0.5, 0.09375, ((0, 2), (1, 16))),
        "down_bias": noise(key_list[9], (D,), 0.3, 1.5, (), jnp.float32),
        "gain_attn": jnp.clip(1.0 + 0.18 * jax.random.normal(key_list[10], (D,), jnp.float32), 0.1, 1.9),
        "shift_attn": noise(key_list[11], (D,), 0.3, 1.5, (), jnp.float32),
        "gain_ffn": jnp.clip(1.0 + 0.18 * jax.random.normal(key_list[12], (D,), jnp.float32), 0.1, 1.9),
        "shift_ffn": noise(key_list[13], (D,), 0.3, 1.5, (), jnp.float32),
        "grad_output": noise(key_list[14], (SEQS, LEN, D), 1.0, 6.0, ((0, 4), (1, 4))),
    }


@jax.custom_vjp
def low(v):
    return lax.optimization_barrier(v.astype(jnp.bfloat16)).astype(jnp.float32)

@jax.custom_vjp
def low_back(v):
    return v

def low_keep(v):
    return (low(v), None)

def low_pass(kept, grad):
    return (grad,)

def back_keep(v):
    return (v, None)

def back_low(kept, grad):
    return (low(grad),)
low.defvjp(low_keep, low_pass)
low_back.defvjp(back_keep, back_low)
EPSILON = 1e-12
NEG_FILL = -1000000000.0
FULL_PRECISION = lax.Precision.HIGHEST

def layer_norm(resid, gain, shift):
    center = resid - lax.optimization_barrier(jnp.mean(resid, -1, keepdims=True))
    spread = lax.optimization_barrier(jnp.mean(center * center, -1, keepdims=True))
    return center * lax.rsqrt(spread + EPSILON) * gain + shift

def project(left_operand, weight_matrix):
    return jnp.einsum('xmn,nf->xmf', left_operand, weight_matrix, precision=FULL_PRECISION)

def forward(usable, inputs, w_qkv, b_qv, w_out, b_out, w_up, b_up, w_down, down_bias, gain_attn, shift_attn, gain_ffn, shift_ffn):
    count, length_value, model_width = inputs.shape
    query = low(low_back(project(inputs, w_qkv[0]) + b_qv[0]))
    key_rows = low(low_back(project(inputs, w_qkv[1])))
    value_rows = low(low_back(project(inputs, w_qkv[2]) + b_qv[1]))
    q_four = query.reshape(count, length_value, HEADS, HEAD_DIM)
    k_four = key_rows.reshape(count, length_value, HEADS, HEAD_DIM)
    v_four = value_rows.reshape(count, length_value, HEADS, HEAD_DIM)
    scores = jnp.einsum('sqhd,skhd->shqk', q_four, k_four, precision=FULL_PRECISION) * HEAD_DIM ** (-0.5)
    scores = low_back(jnp.where(usable[:, None, None, :], scores, NEG_FILL))
    probs = low(jax.nn.softmax(scores, -1))
    attn = jnp.einsum('shqk,skhd->sqhd', probs, v_four, precision=FULL_PRECISION).reshape(count, length_value, model_width)
    attn = low(low_back(attn))
    resid_attn = inputs + low_back(project(attn, w_out)) + b_out
    hidden = layer_norm(resid_attn, gain_attn, shift_attn)
    pre_act = low_back(project(low(hidden), w_up) + b_up)
    activ = low(jax.nn.gelu(pre_act, approximate=False))
    resid_ffn = hidden + low_back(project(activ, w_down)) + down_bias
    return layer_norm(resid_ffn, gain_ffn, shift_ffn)

def reference(inputs, lengths, w_qkv, b_qv, w_out, b_out, w_up, b_up, w_down, down_bias, gain_attn, shift_attn, gain_ffn, shift_ffn, grad_output):
    params = (w_qkv, b_qv, w_out, b_out, w_up, b_up, w_down, down_bias, gain_attn, shift_attn, gain_ffn, shift_ffn)
    params = tuple((p.astype(jnp.float32) for p in params))
    groups = SEQS // SEQ_G
    in_groups = inputs.astype(jnp.float32).reshape(groups, SEQ_G, LEN, D)
    grad_groups = grad_output.astype(jnp.float32).reshape(groups, SEQ_G, LEN, D)
    positions = jnp.arange(LEN, dtype=jnp.int32)
    usable_all = (positions[None, :] < lengths[:, None]).reshape(groups, SEQ_G, LEN)

    def scan_step(summed, sliced):
        group_in, group_gradient, group_usable = sliced

        def local_forward(layer_in, *weights):
            return forward(group_usable, layer_in, *weights)
        result, pullback = jax.vjp(local_forward, group_in, *params)
        grads = pullback(group_gradient)
        summed = tuple((a + b for a, b in zip(summed, grads[1:])))
        return (summed, (result.astype(jnp.bfloat16), grads[0].astype(jnp.bfloat16)))
    zeros = tuple((jnp.zeros_like(p) for p in params))
    summed, (outs_all, grads_all) = lax.scan(scan_step, zeros, (in_groups, grad_groups, usable_all))
    return (outs_all.reshape(SEQS, LEN, D), grads_all.reshape(SEQS, LEN, D), summed[0], summed[1], summed[2], summed[3], summed[4], summed[5], summed[6], summed[7], summed[8], summed[9], summed[10], summed[11])
```

```python
import functools

import jax
import jax.numpy as jnp
from jax import lax
from jax.experimental import pallas as pl
from jax.experimental.pallas import tpu as pltpu
from jax.sharding import PartitionSpec as P

HEAD_DIM = 64
PAIR = 2 * HEAD_DIM
NEG_FILL = -1000000000.0
EPSILON = 1e-12
SCALE = HEAD_DIM ** (-0.5)
BOTH = ("shard", "context")
F32 = jnp.float32
BF16 = jnp.bfloat16


def dot_nn(a, b):
    return jnp.dot(a, b, preferred_element_type=F32)


def dot_nt(a, b):
    return lax.dot_general(a, b, (((1,), (1,)), ((), ())), preferred_element_type=F32)


def dot_tn(a, b):
    return lax.dot_general(a, b, (((0,), (0,)), ((), ())), preferred_element_type=F32)


def lane_half(rows):
    return lax.broadcasted_iota(jnp.int32, (rows, PAIR), 1) < HEAD_DIM


def masked_scores(query, key_head, usable):
    return jnp.where(usable, dot_nt(key_head, query), NEG_FILL)


def forward_kernel(lengths_ref, q_ref, k_ref, v_ref, out_ref, lse_ref):
    length = lengths_ref[pl.program_id(0)]
    count = q_ref.shape[0] * q_ref.shape[2]
    query = q_ref[...].reshape(count, PAIR) * jnp.asarray(SCALE, BF16)
    keys = k_ref[...].reshape(count, PAIR)
    values = v_ref[...].reshape(count, PAIR)
    first = lane_half(count)
    usable = lax.broadcasted_iota(jnp.int32, (count, count), 0) < length
    results = []
    for head in range(2):
        mine = first if head == 0 else jnp.logical_not(first)
        key_head = jnp.where(mine, keys, jnp.zeros_like(keys))
        scores = masked_scores(query, key_head, usable)
        top = jnp.max(scores, 0, keepdims=True)
        weights = jnp.exp(scores - top)
        denom = jnp.sum(weights, 0, keepdims=True)
        lse_ref[0, 0, head : head + 1, :] = top + jnp.log(denom)
        gathered = dot_tn(values, weights.astype(BF16)) * (1.0 / denom)
        results.append(gathered[head * HEAD_DIM : (head + 1) * HEAD_DIM])
    result = jnp.concatenate(results, 0).T
    out_ref[...] = result.astype(BF16).reshape(out_ref.shape)


def backward_kernel(lengths_ref, q_ref, k_ref, v_ref, g_ref, lse_ref, out_ref):
    length = lengths_ref[pl.program_id(0)]
    pair_index = pl.program_id(1)
    pieces, _, piece_len, _ = q_ref.shape
    count = pieces * piece_len
    scale = jnp.asarray(SCALE, BF16)
    query = q_ref[...].reshape(count, PAIR) * scale
    keys = k_ref[...].reshape(count, PAIR)
    values = v_ref[...].reshape(count, PAIR)
    grads = g_ref[...].reshape(count, PAIR)
    scaled_keys = keys * scale
    first = lane_half(count)
    usable = lax.broadcasted_iota(jnp.int32, (count, count), 0) < length
    dquery, dkey, dvalue = [], [], []
    for head in range(2):
        mine = first if head == 0 else jnp.logical_not(first)
        key_head = jnp.where(mine, keys, jnp.zeros_like(keys))
        value_head = jnp.where(mine, values, jnp.zeros_like(values))
        scores = masked_scores(query, key_head, usable)
        probs = jnp.exp(scores - lse_ref[0, 0, head : head + 1, :])
        dprobs = dot_nt(value_head, grads)
        weighted = probs * dprobs
        total = jnp.sum(weighted, 0, keepdims=True)
        dscores = (weighted - probs * total).astype(BF16)
        dvalue.append(dot_nn(probs.astype(BF16), grads))
        dkey.append(dot_nn(dscores, query))
        dquery.append(dot_tn(scaled_keys, dscores)[head * HEAD_DIM : (head + 1) * HEAD_DIM])
    third = out_ref.shape[3] // 3
    block = (pieces, 1, piece_len, PAIR)
    for slot, value in enumerate(
        (
            jnp.concatenate(dquery, 0).T,
            jnp.where(first, dkey[0], dkey[1]),
            jnp.where(first, dvalue[0], dvalue[1]),
        )
    ):
        start = pl.multiple_of(slot * third + pair_index * PAIR, PAIR)
        out_ref[:, :, :, pl.ds(start, PAIR)] = value.astype(BF16).reshape(block)


def attention_specs(shape):
    pieces, _, piece_len, width = shape
    pairs = width // 3 // PAIR
    block = (pieces, 1, piece_len, PAIR)

    def at(offset):
        return pl.BlockSpec(block, lambda s, h: (0, s, 0, offset * pairs + h))

    lse_spec = pl.BlockSpec((1, 1, 2, pieces * piece_len), lambda s, h: (s, h, 0, 0))
    return pairs, at, lse_spec


def attend(lengths, qkv):
    pieces, seqs, piece_len, width = qkv.shape
    count = pieces * piece_len
    pairs, at, lse_spec = attention_specs(qkv.shape)
    return pl.pallas_call(
        forward_kernel,
        grid=(seqs, pairs),
        in_specs=[pl.BlockSpec(memory_space=pltpu.SMEM), at(0), at(1), at(2)],
        out_specs=[at(0), lse_spec],
        out_shape=[
            jax.ShapeDtypeStruct((pieces, seqs, piece_len, width // 3), BF16),
            jax.ShapeDtypeStruct((seqs, pairs, 2, count), F32),
        ],
        compiler_params=pltpu.CompilerParams(vmem_limit_bytes=40 * 1024 * 1024),
        cost_estimate=pl.CostEstimate(
            flops=8 * seqs * pairs * count * count * PAIR,
            bytes_accessed=8 * seqs * pairs * count * PAIR,
            transcendentals=2 * seqs * pairs * count * count,
        ),
    )(lengths, qkv, qkv, qkv)


def attend_back(lengths, qkv, grads, lse):
    pieces, seqs, piece_len, width = qkv.shape
    count = pieces * piece_len
    pairs, at, lse_spec = attention_specs(qkv.shape)
    return pl.pallas_call(
        backward_kernel,
        grid=(seqs, pairs),
        in_specs=[pl.BlockSpec(memory_space=pltpu.SMEM), at(0), at(1), at(2), at(0), lse_spec],
        out_specs=pl.BlockSpec((pieces, 1, piece_len, width), lambda s, h: (0, s, 0, 0)),
        out_shape=jax.ShapeDtypeStruct(qkv.shape, BF16),
        compiler_params=pltpu.CompilerParams(vmem_limit_bytes=40 * 1024 * 1024),
        cost_estimate=pl.CostEstimate(
            flops=20 * seqs * pairs * count * count * PAIR,
            bytes_accessed=14 * seqs * pairs * count * PAIR,
            transcendentals=2 * seqs * pairs * count * count,
        ),
    )(lengths, qkv, qkv, qkv, grads, lse)


def norm_stats(resid):
    center = resid - jnp.mean(resid, -1, keepdims=True)
    inverse = lax.rsqrt(jnp.mean(center * center, -1, keepdims=True) + EPSILON)
    return center * inverse, inverse


def norm_back(normed, inverse, gain, grad):
    scaled = grad * gain
    mean_one = jnp.mean(scaled, -1, keepdims=True)
    mean_two = jnp.mean(scaled * normed, -1, keepdims=True)
    dresid = (scaled - mean_one - normed * mean_two) * inverse
    return dresid, jnp.sum(grad * normed, 0), jnp.sum(grad, 0)


def partner(value):
    return lax.ppermute(value, "tensor", [(0, 1), (1, 0)])


def butterfly(value, sizes):
    for axis, size in sizes:
        bit = 1
        while bit < size:
            value = value + lax.ppermute(value, axis, [(i, i ^ bit) for i in range(size)])
            bit *= 2
    return value


def gather_rows(part):
    return lax.all_gather(part, BOTH, axis=0, tiled=True)


def gelu_parts(pre_act):
    phi_sum = 0.5 * (1.0 + lax.erf(pre_act * (0.5**0.5)))
    density = jnp.exp(-0.5 * pre_act * pre_act) * 0.3989422804014327
    return (pre_act * phi_sum).astype(BF16), (phi_sum + pre_act * density).astype(BF16)


def reduce_rows(own, other):
    summed = (own + partner(other.astype(BF16)).astype(F32)).astype(BF16)
    return lax.psum_scatter(summed, BOTH, scatter_dimension=0, tiled=True).astype(F32)


def on_device(
    sizes,
    inputs,
    lengths,
    w_qkv,
    b_qv,
    w_out,
    b_out,
    w_up,
    b_up,
    w_down,
    down_bias,
    gain_attn,
    shift_attn,
    gain_ffn,
    shift_ffn,
    grad_output,
):
    seq_count, piece_len, model_width = inputs.shape
    pieces = sizes["context"]
    seqs = seq_count // pieces // 2
    rows = pieces * seqs * piece_len
    core = lax.axis_index("tensor")
    group = lax.axis_index("context")
    split = (pieces, 2, seqs, piece_len, model_width)
    four = (pieces, seqs, piece_len)
    axes = (("context", sizes["context"]), ("shard", sizes["shard"]))

    def to_sequences(array):
        half = lax.dynamic_index_in_dim(array.reshape(split), core, 1, keepdims=False)
        return lax.all_to_all(half, "context", split_axis=0, concat_axis=0, tiled=True).reshape(
            rows, model_width
        )

    def to_positions(array):
        own = lax.all_to_all(
            array.reshape(four + (model_width,)), "context", split_axis=0, concat_axis=0, tiled=True
        )
        other = partner(own)
        low = jnp.where(core == 0, own, other)
        high = jnp.where(core == 0, other, own)
        return jnp.stack([low, high], 1).reshape(inputs.shape)

    slots = lengths.reshape(pieces, 2, seqs)
    own_lengths = lax.dynamic_slice(slots, (group, core, 0), (1, 1, seqs)).reshape(seqs)

    head_cols = w_qkv.shape[2]
    qkv_own = gather_rows(w_qkv.transpose(1, 0, 2).reshape(w_qkv.shape[1], 3 * head_cols))
    flat_in = to_sequences(inputs)
    out_own = gather_rows(w_out.T)
    up_own = gather_rows(w_up)
    down_own = gather_rows(w_down.T)
    qkv_other = partner(qkv_own)
    out_other = partner(out_own)
    up_other = partner(up_own)
    down_other = partner(down_own)
    bias_own = jnp.concatenate([b_qv[0], jnp.zeros_like(b_qv[0]), b_qv[1]])
    small_other = partner(jnp.concatenate([bias_own, b_up]))
    bias_other, b_up_other = small_other[: 3 * head_cols], small_other[3 * head_cols :]

    wide = four + (3 * head_cols,)
    proj_own = (dot_nn(flat_in, qkv_own) + bias_own).astype(BF16).reshape(wide)
    attn_own, lse_own = attend(own_lengths, proj_own)
    proj_other = (dot_nn(flat_in, qkv_other) + bias_other).astype(BF16).reshape(wide)
    attn_other, lse_other = attend(own_lengths, proj_other)
    attn_own = attn_own.reshape(rows, head_cols)
    attn_other = attn_other.reshape(rows, head_cols)
    resid_attn = (
        flat_in.astype(F32) + b_out + (dot_nt(attn_own, out_own) + dot_nt(attn_other, out_other))
    )
    normed_attn, inverse_attn = norm_stats(resid_attn)
    hidden = normed_attn * gain_attn + shift_attn
    hidden_low = hidden.astype(BF16)
    activ_own, slope_own = gelu_parts(dot_nn(hidden_low, up_own) + b_up)
    activ_other, slope_other = gelu_parts(dot_nn(hidden_low, up_other) + b_up_other)
    resid_ffn = (
        hidden + down_bias + (dot_nt(activ_own, down_own) + dot_nt(activ_other, down_other))
    )
    normed_ffn, inverse_ffn = norm_stats(resid_ffn)
    outputs = to_positions((normed_ffn * gain_ffn + shift_ffn).astype(BF16))

    grad_flat = to_sequences(grad_output).astype(F32)
    dresid_ffn, grad_gain_ffn, grad_shift_ffn = norm_back(
        normed_ffn, inverse_ffn, gain_ffn, grad_flat
    )
    grad_b_down = jnp.sum(dresid_ffn, 0)
    dbranch_ffn = dresid_ffn.astype(BF16)
    shard_down = reduce_rows(dot_tn(dbranch_ffn, activ_own), dot_tn(dbranch_ffn, activ_other)).T
    dpre_own = (dot_nn(dbranch_ffn, down_own) * slope_own.astype(F32)).astype(BF16)
    dpre_other = (dot_nn(dbranch_ffn, down_other) * slope_other.astype(F32)).astype(BF16)
    shard_up = reduce_rows(dot_tn(hidden_low, dpre_own), dot_tn(hidden_low, dpre_other))
    dhidden = dresid_ffn + (dot_nt(dpre_own, up_own) + dot_nt(dpre_other, up_other))
    dresid_attn, grad_gain_attn, grad_shift_attn = norm_back(
        normed_attn, inverse_attn, gain_attn, dhidden
    )
    grad_b_out = jnp.sum(dresid_attn, 0)
    dbranch_attn = dresid_attn.astype(BF16)
    shard_out = reduce_rows(dot_tn(dbranch_attn, attn_own), dot_tn(dbranch_attn, attn_other)).T

    common = [
        grad_b_out,
        grad_b_down,
        grad_gain_attn,
        grad_shift_attn,
        grad_gain_ffn,
        grad_shift_ffn,
    ]
    up_bias_own = jnp.sum(dpre_own.astype(F32), 0)
    up_bias_other = jnp.sum(dpre_other.astype(F32), 0)
    early = butterfly(
        jnp.concatenate(common + [up_bias_own])
        + partner(jnp.concatenate(common + [up_bias_other])),
        axes,
    )
    sums = early[: 6 * model_width].reshape(6, model_width)
    up_bias_gradient = early[6 * model_width :]

    narrow = four + (head_cols,)
    dattn_own = dot_nn(dbranch_attn, out_own).astype(BF16).reshape(narrow)
    dattn_other = dot_nn(dbranch_attn, out_other).astype(BF16).reshape(narrow)
    dproj_other = attend_back(own_lengths, proj_other, dattn_other, lse_other).reshape(rows, -1)
    dproj_own = attend_back(own_lengths, proj_own, dattn_own, lse_own).reshape(rows, -1)
    shard_qkv = reduce_rows(dot_tn(flat_in, dproj_own), dot_tn(flat_in, dproj_other))
    shard_qkv = shard_qkv.reshape(-1, 3, head_cols).transpose(1, 0, 2)
    grad_inputs = to_positions(
        (dresid_attn + (dot_nt(dproj_own, qkv_own) + dot_nt(dproj_other, qkv_other))).astype(BF16)
    )
    proj_bias_own = jnp.sum(dproj_own.astype(F32), 0)
    proj_bias_other = jnp.sum(dproj_other.astype(F32), 0)
    late = butterfly(proj_bias_own + partner(proj_bias_other), axes).reshape(3, head_cols)
    grad_b_qv = jnp.stack([late[0], late[2]])
    return (
        outputs,
        grad_inputs,
        shard_qkv,
        grad_b_qv,
        shard_out,
        sums[0],
        shard_up,
        up_bias_gradient,
        shard_down,
        sums[1],
        sums[2],
        sums[3],
        sums[4],
        sums[5],
    )


def solution(mesh):
    placed = (
        P("shard", "context", None),
        P("shard"),
        P(None, BOTH, "tensor"),
        P(None, "tensor"),
        P("tensor", BOTH),
        P(),
        P(BOTH, "tensor"),
        P("tensor"),
        P("tensor", BOTH),
        P(),
        P(),
        P(),
        P(),
        P(),
        P("shard", "context", None),
    )
    return jax.shard_map(
        functools.partial(on_device, dict(mesh.shape)),
        mesh=mesh,
        in_specs=placed,
        out_specs=(
            P("shard", "context", None),
            P("shard", "context", None),
            P(None, BOTH, "tensor"),
            P(None, "tensor"),
            P("tensor", BOTH),
            P(),
            P(BOTH, "tensor"),
            P("tensor"),
            P("tensor", BOTH),
            P(),
            P(),
            P(),
            P(),
            P(),
        ),
        check_vma=False,
    )
```

```python
import functools

import jax
import jax.numpy as jnp
from jax import lax
from jax.experimental import pallas as pl
from jax.experimental.pallas import tpu as pltpu
from jax.sharding import PartitionSpec as P

HEAD_DIM = 64
PAIR = 2 * HEAD_DIM
NEG_FILL = -1000000000.0
EPSILON = 1e-12
SCALE = HEAD_DIM ** (-0.5)
BOTH = ("shard", "context")
F32 = jnp.float32
BF16 = jnp.bfloat16


def dot_nn(a, b):
    return jnp.dot(a, b, preferred_element_type=F32)


def dot_nt(a, b):
    return lax.dot_general(a, b, (((1,), (1,)), ((), ())), preferred_element_type=F32)


def dot_tn(a, b):
    return lax.dot_general(a, b, (((0,), (0,)), ((), ())), preferred_element_type=F32)


def lane_half(rows):
    return lax.broadcasted_iota(jnp.int32, (rows, PAIR), 1) < HEAD_DIM


def masked_scores(query, key_head, usable):
    return jnp.where(usable, dot_nt(key_head, query), NEG_FILL)


def forward_kernel(lengths_ref, q_ref, k_ref, v_ref, out_ref, lse_ref):
    length = lengths_ref[pl.program_id(0)]
    count = q_ref.shape[0] * q_ref.shape[2]
    query = q_ref[...].reshape(count, PAIR) * jnp.asarray(SCALE, BF16)
    keys = k_ref[...].reshape(count, PAIR)
    values = v_ref[...].reshape(count, PAIR)
    first = lane_half(count)
    usable = lax.broadcasted_iota(jnp.int32, (count, count), 0) < length
    results = []
    for head in range(2):
        mine = first if head == 0 else jnp.logical_not(first)
        key_head = jnp.where(mine, keys, jnp.zeros_like(keys))
        scores = masked_scores(query, key_head, usable)
        top = jnp.max(scores, 0, keepdims=True)
        weights = jnp.exp(scores - top)
        denom = jnp.sum(weights, 0, keepdims=True)
        lse_ref[0, 0, head : head + 1, :] = top + jnp.log(denom)
        gathered = dot_tn(values, weights.astype(BF16)) * (1.0 / denom)
        results.append(gathered[head * HEAD_DIM : (head + 1) * HEAD_DIM])
    result = jnp.concatenate(results, 0).T
    out_ref[...] = result.astype(BF16).reshape(out_ref.shape)


def backward_kernel(lengths_ref, q_ref, k_ref, v_ref, g_ref, lse_ref, out_ref):
    length = lengths_ref[pl.program_id(0)]
    pair_index = pl.program_id(1)
    pieces, _, piece_len, _ = q_ref.shape
    count = pieces * piece_len
    scale = jnp.asarray(SCALE, BF16)
    query = q_ref[...].reshape(count, PAIR) * scale
    keys = k_ref[...].reshape(count, PAIR)
    values = v_ref[...].reshape(count, PAIR)
    grads = g_ref[...].reshape(count, PAIR)
    scaled_keys = keys * scale
    first = lane_half(count)
    usable = lax.broadcasted_iota(jnp.int32, (count, count), 0) < length
    dquery, dkey, dvalue = [], [], []
    for head in range(2):
        mine = first if head == 0 else jnp.logical_not(first)
        key_head = jnp.where(mine, keys, jnp.zeros_like(keys))
        value_head = jnp.where(mine, values, jnp.zeros_like(values))
        scores = masked_scores(query, key_head, usable)
        probs = jnp.exp(scores - lse_ref[0, 0, head : head + 1, :])
        dprobs = dot_nt(value_head, grads)
        weighted = probs * dprobs
        total = jnp.sum(weighted, 0, keepdims=True)
        dscores = (weighted - probs * total).astype(BF16)
        dvalue.append(dot_nn(probs.astype(BF16), grads))
        dkey.append(dot_nn(dscores, query))
        dquery.append(dot_tn(scaled_keys, dscores)[head * HEAD_DIM : (head + 1) * HEAD_DIM])
    third = out_ref.shape[3] // 3
    block = (pieces, 1, piece_len, PAIR)
    for slot, value in enumerate(
        (
            jnp.concatenate(dquery, 0).T,
            jnp.where(first, dkey[0], dkey[1]),
            jnp.where(first, dvalue[0], dvalue[1]),
        )
    ):
        start = pl.multiple_of(slot * third + pair_index * PAIR, PAIR)
        out_ref[:, :, :, pl.ds(start, PAIR)] = value.astype(BF16).reshape(block)


def attention_specs(shape):
    pieces, _, piece_len, width = shape
    pairs = width // 3 // PAIR
    block = (pieces, 1, piece_len, PAIR)

    def at(offset):
        return pl.BlockSpec(block, lambda s, h: (0, s, 0, offset * pairs + h))

    lse_spec = pl.BlockSpec((1, 1, 2, pieces * piece_len), lambda s, h: (s, h, 0, 0))
    return pairs, at, lse_spec


def attend(lengths, qkv):
    pieces, seqs, piece_len, width = qkv.shape
    count = pieces * piece_len
    pairs, at, lse_spec = attention_specs(qkv.shape)
    return pl.pallas_call(
        forward_kernel,
        grid=(seqs, pairs),
        in_specs=[pl.BlockSpec(memory_space=pltpu.SMEM), at(0), at(1), at(2)],
        out_specs=[at(0), lse_spec],
        out_shape=[
            jax.ShapeDtypeStruct((pieces, seqs, piece_len, width // 3), BF16),
            jax.ShapeDtypeStruct((seqs, pairs, 2, count), F32),
        ],
        compiler_params=pltpu.CompilerParams(vmem_limit_bytes=40 * 1024 * 1024),
        cost_estimate=pl.CostEstimate(
            flops=8 * seqs * pairs * count * count * PAIR,
            bytes_accessed=8 * seqs * pairs * count * PAIR,
            transcendentals=2 * seqs * pairs * count * count,
        ),
    )(lengths, qkv, qkv, qkv)


def attend_back(lengths, qkv, grads, lse):
    pieces, seqs, piece_len, width = qkv.shape
    count = pieces * piece_len
    pairs, at, lse_spec = attention_specs(qkv.shape)
    return pl.pallas_call(
        backward_kernel,
        grid=(seqs, pairs),
        in_specs=[pl.BlockSpec(memory_space=pltpu.SMEM), at(0), at(1), at(2), at(0), lse_spec],
        out_specs=pl.BlockSpec((pieces, 1, piece_len, width), lambda s, h: (0, s, 0, 0)),
        out_shape=jax.ShapeDtypeStruct(qkv.shape, BF16),
        compiler_params=pltpu.CompilerParams(vmem_limit_bytes=40 * 1024 * 1024),
        cost_estimate=pl.CostEstimate(
            flops=20 * seqs * pairs * count * count * PAIR,
            bytes_accessed=14 * seqs * pairs * count * PAIR,
            transcendentals=2 * seqs * pairs * count * count,
        ),
    )(lengths, qkv, qkv, qkv, grads, lse)


def norm_stats(resid):
    center = resid - jnp.mean(resid, -1, keepdims=True)
    inverse = lax.rsqrt(jnp.mean(center * center, -1, keepdims=True) + EPSILON)
    return center * inverse, inverse


def norm_back(normed, inverse, gain, grad):
    scaled = grad * gain
    mean_one = jnp.mean(scaled, -1, keepdims=True)
    mean_two = jnp.mean(scaled * normed, -1, keepdims=True)
    dresid = (scaled - mean_one - normed * mean_two) * inverse
    return dresid, jnp.sum(grad * normed, 0), jnp.sum(grad, 0)


def partner(value):
    return lax.ppermute(value, "tensor", [(0, 1), (1, 0)])


def butterfly(value, sizes):
    for axis, size in sizes:
        bit = 1
        while bit < size:
            value = value + lax.ppermute(value, axis, [(i, i ^ bit) for i in range(size)])
            bit *= 2
    return value


def device_bits(sizes):
    for axis in ("context", "shard"):
        bit = 1
        while bit < sizes[axis]:
            swaps = [(i, i ^ bit) for i in range(sizes[axis])]
            yield axis, swaps, (lax.axis_index(axis) // bit) % 2
            bit *= 2


def gather_doubling(part, sizes):
    for axis, swaps, upper in device_bits(sizes):
        other = lax.ppermute(part, axis, swaps)
        low = jnp.where(upper == 0, part, other)
        high = jnp.where(upper == 0, other, part)
        part = jnp.concatenate([low, high], 0)
    return part


def reduce_halving(own, other, sizes):
    total = own + partner(other.astype(BF16)).astype(F32)
    stages = [total]
    for axis, swaps, upper in reversed(list(device_bits(sizes))):
        halves = total.reshape((2, total.shape[0] // 2) + total.shape[1:])
        kept = lax.dynamic_index_in_dim(halves, upper, 0, keepdims=False)
        sent = lax.dynamic_index_in_dim(halves, 1 - upper, 0, keepdims=False)
        total = kept + lax.ppermute(sent.astype(BF16), axis, swaps).astype(F32)
        stages.append(total)
    return stages


def after(value, *earlier):
    return lax.optimization_barrier((value,) + earlier)[0]


def gather_rows(part):
    return lax.all_gather(part, BOTH, axis=0, tiled=True)


def gelu_parts(pre_act):
    phi_sum = 0.5 * (1.0 + lax.erf(pre_act * (0.5**0.5)))
    density = jnp.exp(-0.5 * pre_act * pre_act) * 0.3989422804014327
    return (pre_act * phi_sum).astype(BF16), (phi_sum + pre_act * density).astype(BF16)


def pair_sum(own, other):
    return (own + partner(other.astype(BF16)).astype(F32)).astype(BF16)


def scatter_rows(summed):
    return lax.psum_scatter(summed, BOTH, scatter_dimension=0, tiled=True).astype(F32)


def on_device(
    sizes,
    inputs,
    lengths,
    w_qkv,
    b_qv,
    w_out,
    b_out,
    w_up,
    b_up,
    w_down,
    down_bias,
    gain_attn,
    shift_attn,
    gain_ffn,
    shift_ffn,
    grad_output,
):
    seq_count, piece_len, model_width = inputs.shape
    pieces = sizes["context"]
    seqs = seq_count // pieces // 2
    rows = pieces * seqs * piece_len
    core = lax.axis_index("tensor")
    group = lax.axis_index("context")
    split = (pieces, 2, seqs, piece_len, model_width)
    four = (pieces, seqs, piece_len)
    axes = (("context", sizes["context"]), ("shard", sizes["shard"]))

    def to_sequences(array):
        half = lax.dynamic_index_in_dim(array.reshape(split), core, 1, keepdims=False)
        return lax.all_to_all(half, "context", split_axis=0, concat_axis=0, tiled=True).reshape(
            rows, model_width
        )

    def to_positions(array):
        own = lax.all_to_all(
            array.reshape(four + (model_width,)), "context", split_axis=0, concat_axis=0, tiled=True
        )
        other = partner(own)
        low = jnp.where(core == 0, own, other)
        high = jnp.where(core == 0, other, own)
        return jnp.stack([low, high], 1).reshape(inputs.shape)

    slots = lengths.reshape(pieces, 2, seqs)
    own_lengths = lax.dynamic_slice(slots, (group, core, 0), (1, 1, seqs)).reshape(seqs)

    head_cols = w_qkv.shape[2]
    qkv_own = gather_rows(w_qkv.transpose(1, 0, 2).reshape(w_qkv.shape[1], 3 * head_cols))
    flat_in = to_sequences(inputs)
    out_own = gather_doubling(w_out.T, sizes)
    up_own = gather_rows(w_up)
    down_own = gather_doubling(w_down.T, sizes)
    qkv_other = partner(qkv_own)
    out_other = partner(out_own)
    bias_own = jnp.concatenate([b_qv[0], jnp.zeros_like(b_qv[0]), b_qv[1]])
    small_other = partner(jnp.concatenate([bias_own, b_up]))
    bias_other, b_up_other = small_other[: 3 * head_cols], small_other[3 * head_cols :]

    wide = four + (3 * head_cols,)
    proj_own = (dot_nn(flat_in, qkv_own) + bias_own).astype(BF16).reshape(wide)
    attn_own, lse_own = attend(own_lengths, proj_own)
    proj_other = (dot_nn(flat_in, qkv_other) + bias_other).astype(BF16).reshape(wide)
    attn_other, lse_other = attend(own_lengths, proj_other)
    up_own = after(up_own, attn_other)
    up_other = partner(up_own)
    down_own = after(down_own, attn_other)
    down_other = partner(down_own)
    attn_own = attn_own.reshape(rows, head_cols)
    attn_other = attn_other.reshape(rows, head_cols)
    resid_attn = (
        flat_in.astype(F32) + b_out + (dot_nt(attn_own, out_own) + dot_nt(attn_other, out_other))
    )
    normed_attn, inverse_attn = norm_stats(resid_attn)
    hidden = normed_attn * gain_attn + shift_attn
    hidden_low = hidden.astype(BF16)
    activ_own, slope_own = gelu_parts(dot_nn(hidden_low, up_own) + b_up)
    activ_other, slope_other = gelu_parts(dot_nn(hidden_low, up_other) + b_up_other)
    resid_ffn = (
        hidden + down_bias + (dot_nt(activ_own, down_own) + dot_nt(activ_other, down_other))
    )
    normed_ffn, inverse_ffn = norm_stats(resid_ffn)
    outputs = to_positions((normed_ffn * gain_ffn + shift_ffn).astype(BF16))

    grad_flat = to_sequences(after(grad_output, proj_own)).astype(F32)
    dresid_ffn, grad_gain_ffn, grad_shift_ffn = norm_back(
        normed_ffn, inverse_ffn, gain_ffn, grad_flat
    )
    grad_b_down = jnp.sum(dresid_ffn, 0)
    dbranch_ffn = dresid_ffn.astype(BF16)
    down_stages = reduce_halving(
        dot_tn(dbranch_ffn, activ_own), dot_tn(dbranch_ffn, activ_other), sizes
    )
    shard_down = down_stages[-1].T
    dpre_own = (dot_nn(dbranch_ffn, down_own) * slope_own.astype(F32)).astype(BF16)
    dpre_other = (dot_nn(dbranch_ffn, down_other) * slope_other.astype(F32)).astype(BF16)
    summed_up = pair_sum(dot_tn(hidden_low, dpre_own), dot_tn(hidden_low, dpre_other))
    shard_up = scatter_rows(summed_up)
    dhidden = dresid_ffn + (dot_nt(dpre_own, up_own) + dot_nt(dpre_other, up_other))
    dresid_attn, grad_gain_attn, grad_shift_attn = norm_back(
        normed_attn, inverse_attn, gain_attn, dhidden
    )
    grad_b_out = jnp.sum(dresid_attn, 0)
    dbranch_attn = dresid_attn.astype(BF16)
    out_stages = reduce_halving(
        dot_tn(dbranch_attn, attn_own), dot_tn(dbranch_attn, attn_other), sizes
    )
    shard_out = out_stages[-1].T

    common = [
        grad_b_out,
        grad_b_down,
        grad_gain_attn,
        grad_shift_attn,
        grad_gain_ffn,
        grad_shift_ffn,
    ]
    up_bias_own = jnp.sum(dpre_own.astype(F32), 0)
    up_bias_other = jnp.sum(dpre_other.astype(F32), 0)
    early = butterfly(
        jnp.concatenate(common + [up_bias_own])
        + partner(jnp.concatenate(common + [up_bias_other])),
        axes,
    )
    sums = early[: 6 * model_width].reshape(6, model_width)
    up_bias_gradient = early[6 * model_width :]

    narrow = four + (head_cols,)
    dattn_own = dot_nn(dbranch_attn, out_own).astype(BF16).reshape(narrow)
    dattn_other = dot_nn(dbranch_attn, out_other).astype(BF16).reshape(narrow)
    dattn_other = after(dattn_other, summed_up)
    dattn_own = after(dattn_own, down_stages[0])
    dproj_other = attend_back(own_lengths, proj_other, dattn_other, lse_other).reshape(rows, -1)
    dproj_own = attend_back(own_lengths, proj_own, dattn_own, lse_own).reshape(rows, -1)
    dproj_own = after(dproj_own, outputs, down_stages[2])
    summed_qkv = pair_sum(dot_tn(flat_in, dproj_own), dot_tn(flat_in, dproj_other))
    shard_qkv = scatter_rows(after(summed_qkv, shard_up))
    shard_qkv = shard_qkv.reshape(-1, 3, head_cols).transpose(1, 0, 2)
    grad_inputs = to_positions(
        (dresid_attn + (dot_nt(dproj_own, qkv_own) + dot_nt(dproj_other, qkv_other))).astype(BF16)
    )
    proj_bias_own = jnp.sum(dproj_own.astype(F32), 0)
    proj_bias_other = jnp.sum(dproj_other.astype(F32), 0)
    late = butterfly(proj_bias_own + partner(proj_bias_other), axes).reshape(3, head_cols)
    grad_b_qv = jnp.stack([late[0], late[2]])
    return (
        outputs,
        grad_inputs,
        shard_qkv,
        grad_b_qv,
        shard_out,
        sums[0],
        shard_up,
        up_bias_gradient,
        shard_down,
        sums[1],
        sums[2],
        sums[3],
        sums[4],
        sums[5],
    )


def solution(mesh):
    placed = (
        P("shard", "context", None),
        P("shard"),
        P(None, BOTH, "tensor"),
        P(None, "tensor"),
        P("tensor", BOTH),
        P(),
        P(BOTH, "tensor"),
        P("tensor"),
        P("tensor", BOTH),
        P(),
        P(),
        P(),
        P(),
        P(),
        P("shard", "context", None),
    )
    return jax.shard_map(
        functools.partial(on_device, dict(mesh.shape)),
        mesh=mesh,
        in_specs=placed,
        out_specs=(
            P("shard", "context", None),
            P("shard", "context", None),
            P(None, BOTH, "tensor"),
            P(None, "tensor"),
            P("tensor", BOTH),
            P(),
            P(BOTH, "tensor"),
            P("tensor"),
            P("tensor", BOTH),
            P(),
            P(),
            P(),
            P(),
            P(),
        ),
        check_vma=False,
    )
```
